32 devices in a mesh: row: 4 (over y, core), src: 8 (over z, x).
Axes of the slice: x: 2, y: 2, z: 4, core: 2. Of those that a mesh axis runs over, the one named last changes fastest.
Arguments:
- front_panel: float32 [3, 256, 8192], P(None, None, ('row', 'src')), may hold values from -0.0625 to 0.0625
- solved_prev: float32 [8192, 2048], P('row', 'src'), may hold values from -6 to 6
- right_side: float32 [768, 2048], P(None, 'src'), may hold values from -6 to 6
- front_window: float32 [768, 768], replicated, may hold values from -0.21875 to 0.21875
- inv_diag: float32 [3, 256, 256], replicated, may hold values from -0.375 to 0.375
- owner_map: int32 [3], replicated, may hold values from 0 to 3, as said below
Outputs:
- stored: float32 [1024, 2048], P('row', 'src')
The draws below stay inside these ranges and needn't reach their ends.
Inputs may be any that keep to these rules, and one draw needn't show every extreme that they name: `owner_map`: the blocks' owners are distinct row groups.
All inputs are finite; a program needn't handle non-finite values.
Results may differ from the reference program's by a relative error of at most 0.0001.
Values sent between devices are 32-bit elements; how exact they have to be, the bound alone decides.
A program may use at most 64 MiB of HBM per device.

```python
import jax
import jax.numpy as jnp
from jax import lax

NB = 256
NBLK = 3
WIN = 768
PREV = 8192
SOURCES = 2048
N_ROW = 4


def draw_owner_map(key, part):
    middle = jax.random.permutation(jax.random.fold_in(key, 7), N_ROW - 2).astype(jnp.int32) + 1
    ends = jnp.array([0, N_ROW - 1], jnp.int32)
    chosen = jnp.concatenate([ends, middle[:NBLK - 2]])
    return jax.random.permutation(jax.random.fold_in(key, 11), chosen).astype(jnp.int32)


def steps_of(rng, shape, cuts, smallest, high):
    gain, own = 1.0, jax.random.fold_in(rng, 6)
    for dim, shards_of in cuts:
        heights = jnp.exp(jax.random.uniform(jax.random.fold_in(own, dim), (shards_of,), jnp.float32, smallest / len(cuts), high / len(cuts)))
        gain = gain * jnp.repeat(heights, shape[dim] // shards_of).reshape([-1 if axis == dim else 1 for axis in range(len(shape))])
    return gain


def normal_values(key, extent, scale, limit, cuts=(), kind=jnp.bfloat16):
    drawn = jax.random.normal(key, extent, jnp.float32) * scale
    if len(cuts) > 0:
        drawn = steps_of(key, extent, cuts, -0.22, 0.18) * drawn
    return jnp.clip(drawn, min=-limit, max=limit).astype(kind)


def setup_inputs(seed: int = 0) -> dict:
    arg_keys = jax.random.split(jax.random.key(seed), 7)
    front_panel = normal_values(arg_keys[0], (NBLK, NB, PREV), PREV ** -0.5, 0.0625, ((2, 32),), jnp.float32)
    solved_prev = normal_values(arg_keys[1], (PREV, SOURCES), 1.0, 6.0, ((0, 4), (1, 8)), jnp.float32)
    right_side = normal_values(arg_keys[2], (WIN, SOURCES), 1.0, 6.0, ((1, 8),), jnp.float32)
    front_window = normal_values(arg_keys[3], (WIN, WIN), WIN ** -0.5, 0.21875, (), jnp.float32)
    inv_diag = normal_values(arg_keys[4], (NBLK, NB, NB), NB ** -0.5, 0.375, (), jnp.float32)
    owner_map = draw_owner_map(jax.random.fold_in(arg_keys[6], 71), 0)
    return dict(front_panel=front_panel, solved_prev=solved_prev, right_side=right_side, front_window=front_window, inv_diag=inv_diag, owner_map=owner_map)


def reference(front_panel, solved_prev, right_side, front_window, inv_diag, owner_map):
    highest = lax.Precision.HIGHEST
    stored = jnp.zeros((N_ROW * NB, right_side.shape[1]), jnp.float32)
    solutions = []
    for k in range(NBLK):
        partial_value = jnp.dot(front_panel[k], solved_prev, precision=highest, preferred_element_type=jnp.float32)
        rhs = right_side[k * NB:(k + 1) * NB] - partial_value
        if k > 0:
            earlier = jnp.concatenate(solutions, axis=0)
            rhs = rhs - jnp.dot(front_window[k * NB:(k + 1) * NB, :k * NB], earlier, precision=highest, preferred_element_type=jnp.float32)
        solution = jnp.dot(inv_diag[k], rhs, precision=highest, preferred_element_type=jnp.float32)
        solutions.append(solution)
        start = (owner_map[k] * NB).astype(jnp.int32)
        stored = lax.dynamic_update_slice(stored, solution, (start, jnp.int32(0)))
    return stored
```

```python
import functools

import jax
import jax.numpy as jnp
from jax import lax
from jax.experimental import pallas as pl
from jax.experimental.pallas import tpu as pltpu
from jax.sharding import PartitionSpec as P

F32 = jnp.float32
BF16 = jnp.bfloat16
MESH = pl.DeviceIdType.MESH


def general_body(front_panel, solved_prev, right_side, front_window, inv_diag, owner_map):
    highest = lax.Precision.HIGHEST
    nblk = front_panel.shape[0]
    block = front_panel.shape[1]
    width = solved_prev.shape[1]
    here = lax.axis_index("row")
    panel_rows = lax.all_gather(front_panel, "src", axis=2, tiled=True)
    local = jnp.einsum(
        "kbn,ns->kbs",
        panel_rows,
        solved_prev,
        precision=highest,
        preferred_element_type=jnp.float32,
    )
    partials = lax.psum(local, "row")
    stored = jnp.zeros((block, width), jnp.float32)
    solutions = []
    for k in range(nblk):
        rhs = right_side[k * block : (k + 1) * block] - partials[k]
        if k > 0:
            earlier = jnp.concatenate(solutions, axis=0)
            rhs = rhs - jnp.dot(
                front_window[k * block : (k + 1) * block, : k * block],
                earlier,
                precision=highest,
                preferred_element_type=jnp.float32,
            )
        mine = here == owner_map[k]
        solution = jnp.dot(inv_diag[k], rhs, precision=highest, preferred_element_type=jnp.float32)
        solutions.append(solution)
        stored = stored + jnp.where(mine, solution, jnp.zeros_like(solution))
    return stored


def split(v):
    hi = v.astype(BF16)
    return hi, (v - hi.astype(F32)).astype(BF16)


def dot(a, b):
    return jnp.dot(a, b, preferred_element_type=F32)


def dot3(a, b):
    (ah, al), (bh, bl) = split(a), split(b)
    return dot(ah, bh) + (dot(ah, bl) + dot(al, bh))


def kernel(
    nz, n_row, owner, fp, sp, rs, win, inv, out,
    ga, rb, bh, bl, ah, al, acc, rc, sx, rx, ty, ry, fs, fr,
    zr_send, zl_send, z_recv, b_send, b_recv, c_send, c_recv, x_send, x_recv, y_send, y_recv, f_sem,
):
    nblk, block, kc = fp.shape
    width = sp.shape[1]
    half = width // 2
    row, src = lax.axis_index("row"), lax.axis_index("src")
    z, x = src // 2, lax.rem(src, 2)
    core = lax.rem(row, 2)
    sib = row + 1 - 2 * core
    yp = lax.rem(row + 2, n_row)
    xp = src + 1 - 2 * x
    has_l, has_r = z > 0, z < nz - 1

    to_sib = {"row": sib, "src": src}
    to_y = {"row": yp, "src": src}
    to_x = {"row": row, "src": xp}
    to_r = {"row": row, "src": src + 2}
    to_l = {"row": row, "src": src - 2}

    def remote(s, d, ss, rr, dev):
        return pltpu.make_async_remote_copy(
            src_ref=s, dst_ref=d, send_sem=ss, recv_sem=rr, device_id=dev, device_id_type=MESH
        )

    barrier = pltpu.get_barrier_semaphore()

    def hello(dev):
        pl.semaphore_signal(barrier, inc=1, device_id=dev, device_id_type=MESH)

    for dev in (to_sib, to_y, to_x):
        hello(dev)
    pl.when(has_l)(lambda: hello(to_l))
    pl.when(has_r)(lambda: hello(to_r))
    pl.semaphore_wait(barrier, 3 + has_l.astype(jnp.int32) + has_r.astype(jnp.int32))

    def right(k, o, own):
        s = fp.at[k] if own else ga.at[k, o]
        return remote(s, ga.at[k, o], zr_send.at[k, o], z_recv.at[k, o], to_r)

    def left(k, o, own):
        s = fp.at[k] if own else ga.at[k, o]
        return remote(s, ga.at[k, o], zl_send.at[k, o], z_recv.at[k, o], to_l)

    def send_own(k):
        pl.when(has_r)(lambda: right(k, z, True).start())
        pl.when(has_l)(lambda: left(k, z, True).start())

    def rows_of(o, par):
        return pl.ds(pl.multiple_of((2 * o + par) * kc, kc), kc)

    def b_copy(o):
        return remote(sp.at[rows_of(o, 1 - x)], rb.at[o], b_send.at[o], b_recv.at[o], to_x)

    def passing(k, d):
        @pl.when(z - d >= 0)
        def _():
            right(k, z - d, False).wait_recv()
            pl.when(has_r)(lambda: right(k, z - d, False).start())

        @pl.when(z + d < nz)
        def _():
            left(k, z + d, False).wait_recv()
            pl.when(has_l)(lambda: left(k, z + d, False).start())

    def c_copy(k):
        return remote(acc.at[k, 1 - core], rc.at[k], c_send.at[k], c_recv.at[k], to_sib)

    def x_copy(k):
        return remote(sx.at[k, 1], rx.at[k], x_send.at[k], x_recv.at[k], to_x)

    def y_copy(k):
        return remote(ty.at[k], ry.at[k], y_send.at[k], y_recv.at[k], to_y)

    send_own(0)
    for o in range(nz):
        b_copy(o).start()
    if nblk > 1:
        send_own(1)
    for k in range(nblk):
        ga[k, z] = fp[k]
    for o in range(nz):
        hi, lo = split(sp[rows_of(o, x), :])
        bh[0, o * kc : (o + 1) * kc] = hi
        bl[0, o * kc : (o + 1) * kc] = lo

    cols = pl.ds(pl.multiple_of(core * half, half), half)
    other = pl.ds(pl.multiple_of((1 - core) * half, half), half)
    solutions = []

    def stage_core(k):
        c_copy(k).wait_recv()
        sx[k, 1] = acc[k, core, 1] + rc[k, 1]
        x_copy(k).start()
        sx[k, 0] = acc[k, core, 0] + rc[k, 0]

    def stage_x(k):
        x_copy(k).wait_recv()
        ty[k] = sx[k, 0] + rx[k]
        y_copy(k).start()
        rhs = rs[k * block : (k + 1) * block, cols]
        for j in range(k):
            rhs = rhs - dot3(win[k * block : (k + 1) * block, j * block : (j + 1) * block], solutions[j])
        return rhs

    def stage_y(k, rhs):
        y_copy(k).wait_recv()
        solutions.append(dot3(inv[k], rhs - (ty[k] + ry[k])))

    for k in range(nblk):
        if k > 0 and k + 1 < nblk:
            send_own(k + 1)
        rhs = None
        for d in range(1, max(nz, 4)):
            if d < nz:
                passing(k, d)
            if k > 0:
                if d == 1:
                    stage_core(k - 1)
                elif d == 2:
                    rhs = stage_x(k - 1)
                elif d == 3:
                    stage_y(k - 1, rhs)
        if k == 0:
            for o in range(nz):
                b_copy(o).wait_recv()
                hi, lo = split(rb[o])
                bh[1, o * kc : (o + 1) * kc] = hi
                bl[1, o * kc : (o + 1) * kc] = lo
        for o in range(nz):
            hi, lo = split(ga[k, o])
            ah[:, o * kc : (o + 1) * kc] = hi
            al[:, o * kc : (o + 1) * kc] = lo
        for g in range(2):
            p = dot(ah[...], bh[g]) + (dot(ah[...], bl[g]) + dot(al[...], bh[g]))
            acc[k, 0, g] = p[:, :half]
            acc[k, 1, g] = p[:, half:]
        c_copy(k).start()

    last = nblk - 1
    stage_core(last)
    stage_y(last, stage_x(last))

    def pick(r):
        total = jnp.zeros((block, half), F32)
        for k in range(nblk):
            total = total + jnp.where(owner[k] == r, solutions[k], jnp.zeros_like(total))
        return total

    fs[...] = pick(sib)
    final = remote(fs, fr, f_sem.at[0], f_sem.at[1], to_sib)
    final.start()
    out[:, cols] = pick(row)

    for k in range(nblk):
        for o in range(nz):
            pl.when(has_r & (o <= z))(lambda: right(k, o, False).wait_send())
            pl.when(has_l & (o >= z))(lambda: left(k, o, False).wait_send())
        c_copy(k).wait_send()
        x_copy(k).wait_send()
        y_copy(k).wait_send()
    for o in range(nz):
        b_copy(o).wait_send()
    final.wait()
    out[:, other] = fr[...]


def fast_body(n_row, n_src, front_panel, solved_prev, right_side, front_window, inv_diag, owner_map):
    nblk, block, kc = front_panel.shape
    width = solved_prev.shape[1]
    nz, half = n_src // 2, width // 2
    vmem = pl.BlockSpec(memory_space=pltpu.VMEM)
    dma = pltpu.SemaphoreType.DMA
    return pl.pallas_call(
        functools.partial(kernel, nz, n_row),
        out_shape=jax.ShapeDtypeStruct((block, width), F32),
        in_specs=[pl.BlockSpec(memory_space=pltpu.SMEM)] + [vmem] * 5,
        out_specs=vmem,
        scratch_shapes=[
            pltpu.VMEM((nblk, nz, block, kc), F32),
            pltpu.VMEM((nz, kc, width), F32),
            pltpu.VMEM((2, nz * kc, width), BF16),
            pltpu.VMEM((2, nz * kc, width), BF16),
            pltpu.VMEM((block, nz * kc), BF16),
            pltpu.VMEM((block, nz * kc), BF16),
            pltpu.VMEM((nblk, 2, 2, block, half), F32),
            pltpu.VMEM((nblk, 2, block, half), F32),
            pltpu.VMEM((nblk, 2, block, half), F32),
            pltpu.VMEM((nblk, block, half), F32),
            pltpu.VMEM((nblk, block, half), F32),
            pltpu.VMEM((nblk, block, half), F32),
            pltpu.VMEM((block, half), F32),
            pltpu.VMEM((block, half), F32),
            dma((nblk, nz)),
            dma((nblk, nz)),
            dma((nblk, nz)),
            dma((nz,)),
            dma((nz,)),
            dma((nblk,)),
            dma((nblk,)),
            dma((nblk,)),
            dma((nblk,)),
            dma((nblk,)),
            dma((nblk,)),
            dma((2,)),
        ],
        compiler_params=pltpu.CompilerParams(
            collective_id=0, has_side_effects=True, vmem_limit_bytes=48 * 2**20
        ),
    )(owner_map, front_panel, solved_prev, right_side, front_window, inv_diag)


def solution(mesh):
    n_row, n_src = mesh.shape["row"], mesh.shape["src"]

    def body(front_panel, solved_prev, *rest):
        nblk, block, kc = front_panel.shape
        width = solved_prev.shape[1]
        fits = n_row == 4 and n_src % 2 == 0 and n_src >= 4 and n_src <= 16
        fits = fits and block % 16 == 0 and kc % 128 == 0 and width % 256 == 0
        if fits:
            return fast_body(n_row, n_src, front_panel, solved_prev, *rest)
        return general_body(front_panel, solved_prev, *rest)

    in_specs = (P(None, None, ("row", "src")), P("row", "src"), P(None, "src"), P(), P(), P())
    out_specs = P("row", "src")
    return jax.shard_map(body, mesh=mesh, in_specs=in_specs, out_specs=out_specs, check_vma=False)
```

```python
import functools

import jax
import jax.numpy as jnp
from jax import lax
from jax.experimental import pallas as pl
from jax.experimental.pallas import tpu as pltpu
from jax.sharding import PartitionSpec as P

F32 = jnp.float32
BF16 = jnp.bfloat16
MESH = pl.DeviceIdType.MESH


def general_body(front_panel, solved_prev, right_side, front_window, inv_diag, owner_map):
    highest = lax.Precision.HIGHEST
    nblk = front_panel.shape[0]
    block = front_panel.shape[1]
    width = solved_prev.shape[1]
    here = lax.axis_index("row")
    panel_rows = lax.all_gather(front_panel, "src", axis=2, tiled=True)
    local = jnp.einsum(
        "kbn,ns->kbs",
        panel_rows,
        solved_prev,
        precision=highest,
        preferred_element_type=jnp.float32,
    )
    partials = lax.psum(local, "row")
    stored = jnp.zeros((block, width), jnp.float32)
    solutions = []
    for k in range(nblk):
        rhs = right_side[k * block : (k + 1) * block] - partials[k]
        if k > 0:
            earlier = jnp.concatenate(solutions, axis=0)
            rhs = rhs - jnp.dot(
                front_window[k * block : (k + 1) * block, : k * block],
                earlier,
                precision=highest,
                preferred_element_type=jnp.float32,
            )
        mine = here == owner_map[k]
        solution = jnp.dot(inv_diag[k], rhs, precision=highest, preferred_element_type=jnp.float32)
        solutions.append(solution)
        stored = stored + jnp.where(mine, solution, jnp.zeros_like(solution))
    return stored


def split(v):
    hi = v.astype(BF16)
    return hi, (v - hi.astype(F32)).astype(BF16)


def dot(a, b):
    return jnp.dot(a, b, preferred_element_type=F32)


def dot3(a, b):
    (ah, al), (bh, bl) = split(a), split(b)
    return dot(ah, bh) + (dot(ah, bl) + dot(al, bh))


def kernel(
    nz, n_row, cut, owner, fp, sp, rs_hbm, win_hbm, inv_hbm, out,
    ga, rb, sv, rs, win, inv, bh, bl, acc, rc, sx, rx, ty, ry, fs, fr,
    zr_send, zl_send, z_recv, b_send, b_recv, c_send, c_recv, x_send, x_recv, y_send, y_recv, f_sem, l_sem, g_sem, s_sem,
):
    pieces, rows, kc = fp.shape
    width = sp.shape[1]
    half = width // 2
    nblk = pieces // cut
    block = rows * cut
    row, src = lax.axis_index("row"), lax.axis_index("src")
    z, x = src // 2, lax.rem(src, 2)
    core = lax.rem(row, 2)
    sib = row + 1 - 2 * core
    yp = lax.rem(row + 2, n_row)
    xp = src + 1 - 2 * x
    has_l, has_r = z > 0, z < nz - 1

    to_sib = {"row": sib, "src": src}
    to_y = {"row": yp, "src": src}
    to_x = {"row": row, "src": xp}
    to_r = {"row": row, "src": src + 2}
    to_l = {"row": row, "src": src - 2}

    def remote(s, d, ss, rr, dev):
        return pltpu.make_async_remote_copy(
            src_ref=s, dst_ref=d, send_sem=ss, recv_sem=rr, device_id=dev, device_id_type=MESH
        )

    def rows_of(o, par):
        return pl.ds(pl.multiple_of((2 * o + par) * kc, kc), kc)

    def own_copy(p):
        return pltpu.make_async_copy(fp.at[p], ga.at[p, z], g_sem.at[p])

    def sv_copy(o):
        return pltpu.make_async_copy(sp.at[rows_of(o, x)], sv.at[o], s_sem.at[o])

    small = [
        pltpu.make_async_copy(rs_hbm, rs, l_sem.at[0]),
        pltpu.make_async_copy(win_hbm, win, l_sem.at[1]),
        pltpu.make_async_copy(inv_hbm, inv, l_sem.at[2]),
    ]

    barrier = pltpu.get_barrier_semaphore()

    def hello(dev):
        pl.semaphore_signal(barrier, inc=1, device_id=dev, device_id_type=MESH)

    for dev in (to_sib, to_y, to_x):
        hello(dev)
    pl.when(has_l)(lambda: hello(to_l))
    pl.when(has_r)(lambda: hello(to_r))
    for o in range(nz):
        sv_copy(o).start()
    for p in range(pieces):
        own_copy(p).start()
    for copy in small:
        copy.start()
    pl.semaphore_wait(barrier, 3 + has_l.astype(jnp.int32) + has_r.astype(jnp.int32))

    def right(p, o, own=False):
        s = fp.at[p] if own else ga.at[p, o]
        return remote(s, ga.at[p, o], zr_send.at[p, o], z_recv.at[p, o], to_r)

    def left(p, o, own=False):
        s = fp.at[p] if own else ga.at[p, o]
        return remote(s, ga.at[p, o], zl_send.at[p, o], z_recv.at[p, o], to_l)

    def b_copy(o):
        return remote(sp.at[rows_of(o, 1 - x)], rb.at[o], b_send.at[o], b_recv.at[o], to_x)

    def passing(p, d):
        @pl.when(z - d >= 0)
        def _():
            right(p, z - d).wait_recv()
            pl.when(has_r)(lambda: right(p, z - d).start())

        @pl.when(z + d < nz)
        def _():
            left(p, z + d).wait_recv()
            pl.when(has_l)(lambda: left(p, z + d).start())

    def each(body):
        lax.fori_loop(0, pieces, lambda p, c: (body(p), c)[1], 0)

    for p in range(pieces):
        pl.when(has_r)(lambda p=p: right(p, z, True).start())
        pl.when(has_l)(lambda p=p: left(p, z, True).start())
        if p < nz:
            b_copy(p).start()
    for o in range(pieces, nz):
        b_copy(o).start()

    for o in range(nz):
        sv_copy(o).wait()
        hi, lo = split(sv[o])
        bh[0, o * kc : (o + 1) * kc] = hi
        bl[0, o * kc : (o + 1) * kc] = lo

    each(lambda p: passing(p, 1))
    for copy in small:
        copy.wait()
    for o in range(nz):
        b_copy(o).wait_recv()
        hi, lo = split(rb[o])
        bh[1, o * kc : (o + 1) * kc] = hi
        bl[1, o * kc : (o + 1) * kc] = lo

    def product(p, o, first=False):
        hi, lo = split(ga[p, o])
        at = pl.ds(pl.multiple_of(o * kc, kc), kc)
        for g in range(2):
            t = dot(hi, bh[g, at]) + (dot(hi, bl[g, at]) + dot(lo, bh[g, at]))
            if first:
                acc[p, 0, g] = t[:, :half]
                acc[p, 1, g] = t[:, half:]
            else:
                acc[p, 0, g] += t[:, :half]
                acc[p, 1, g] += t[:, half:]

    def own_product(p):
        own_copy(p).wait()
        product(p, z, True)

    def products(p, d):
        if 2 * d >= nz:
            some = (z - d >= 0) | (z + d < nz)
            pl.when(some)(lambda: product(p, jnp.where(z - d >= 0, z - d, z + d)))
        else:
            pl.when(z - d >= 0)(lambda: product(p, z - d))
            pl.when(z + d < nz)(lambda: product(p, z + d))

    each(own_product)
    each(lambda p: products(p, 1))
    for d in range(2, nz - 1):

        def both(p, d=d):
            passing(p, d)
            products(p, d)

        each(both)

    def c_copy(p):
        return remote(acc.at[p, 1 - core], rc.at[p], c_send.at[p], c_recv.at[p], to_sib)

    def x_copy(p):
        return remote(sx.at[p, 1], rx.at[p], x_send.at[p], x_recv.at[p], to_x)

    def y_copy(p):
        return remote(ty.at[p], ry.at[p], y_send.at[p], y_recv.at[p], to_y)

    cols = pl.ds(pl.multiple_of(core * half, half), half)
    other = pl.ds(pl.multiple_of((1 - core) * half, half), half)
    solutions = []
    rhs = [None]

    def stage_core(p):
        c_copy(p).wait_recv()
        sx[p, 1] = acc[p, core, 1] + rc[p, 1]
        x_copy(p).start()
        sx[p, 0] = acc[p, core, 0] + rc[p, 0]

    def stage_x(p):
        x_copy(p).wait_recv()
        ty[p] = sx[p, 0] + rx[p]
        y_copy(p).start()

    def prepare(k):
        v = rs[k * block : (k + 1) * block, cols]
        for j in range(k):
            v = v - dot3(win[k * block : (k + 1) * block, j * block : (j + 1) * block], solutions[j])
        return v

    def stage_y(p):
        y_copy(p).wait_recv()
        if p % cut == cut - 1:
            k = p // cut
            total = jnp.concatenate([ty[q] + ry[q] for q in range(k * cut, p + 1)], axis=0)
            solutions.append(dot3(inv[k], (rhs[0] if rhs[0] is not None else prepare(k)) - total))
            rhs[0] = prepare(k + 1) if k + 1 < nblk else None

    for step in range(pieces + 3):
        if step < pieces:
            if nz > 2:
                passing(step, nz - 1)
                products(step, nz - 1)
            c_copy(step).start()
        if 0 <= step - 1 < pieces:
            stage_core(step - 1)
        if 0 <= step - 2 < pieces:
            stage_x(step - 2)
        if 0 <= step - 3 < pieces:
            stage_y(step - 3)

    def pick(r):
        total = jnp.zeros((block, half), F32)
        for k in range(nblk):
            total = total + jnp.where(owner[k] == r, solutions[k], jnp.zeros_like(total))
        return total

    fs[...] = pick(sib)
    final = remote(fs, fr, f_sem.at[0], f_sem.at[1], to_sib)
    final.start()
    out[:, cols] = pick(row)

    def settle(p):
        for o in range(nz):
            pl.when(has_r & (o <= z))(lambda o=o: right(p, o).wait_send())
            pl.when(has_l & (o >= z))(lambda o=o: left(p, o).wait_send())
        c_copy(p).wait_send()
        x_copy(p).wait_send()
        y_copy(p).wait_send()

    each(settle)
    for o in range(nz):
        b_copy(o).wait_send()
    final.wait()
    out[:, other] = fr[...]


def fast_body(n_row, n_src, front_panel, solved_prev, right_side, front_window, inv_diag, owner_map):
    nblk, block, kc = front_panel.shape
    width = solved_prev.shape[1]
    nz, half = n_src // 2, width // 2
    cut = 2
    pieces, rows = nblk * cut, block // cut
    hbm = pl.BlockSpec(memory_space=pl.ANY)
    dma = pltpu.SemaphoreType.DMA
    return pl.pallas_call(
        functools.partial(kernel, nz, n_row, cut),
        out_shape=jax.ShapeDtypeStruct((block, width), F32),
        in_specs=[pl.BlockSpec(memory_space=pltpu.SMEM)] + [hbm] * 5,
        out_specs=pl.BlockSpec(memory_space=pltpu.VMEM),
        scratch_shapes=[
            pltpu.VMEM((pieces, nz, rows, kc), F32),
            pltpu.VMEM((nz, kc, width), F32),
            pltpu.VMEM((nz, kc, width), F32),
            pltpu.VMEM(right_side.shape, F32),
            pltpu.VMEM(front_window.shape, F32),
            pltpu.VMEM(inv_diag.shape, F32),
            pltpu.VMEM((2, nz * kc, width), BF16),
            pltpu.VMEM((2, nz * kc, width), BF16),
            pltpu.VMEM((pieces, 2, 2, rows, half), F32),
            pltpu.VMEM((pieces, 2, rows, half), F32),
            pltpu.VMEM((pieces, 2, rows, half), F32),
            pltpu.VMEM((pieces, rows, half), F32),
            pltpu.VMEM((pieces, rows, half), F32),
            pltpu.VMEM((pieces, rows, half), F32),
            pltpu.VMEM((block, half), F32),
            pltpu.VMEM((block, half), F32),
            dma((pieces, nz)),
            dma((pieces, nz)),
            dma((pieces, nz)),
            dma((nz,)),
            dma((nz,)),
            dma((pieces,)),
            dma((pieces,)),
            dma((pieces,)),
            dma((pieces,)),
            dma((pieces,)),
            dma((pieces,)),
            dma((2,)),
            dma((3,)),
            dma((pieces,)),
            dma((nz,)),
        ],
        compiler_params=pltpu.CompilerParams(
            collective_id=0, has_side_effects=True, vmem_limit_bytes=56 * 2**20
        ),
    )(
        owner_map, front_panel.reshape(pieces, rows, kc), solved_prev, right_side, front_window, inv_diag
    )


def solution(mesh):
    n_row, n_src = mesh.shape["row"], mesh.shape["src"]

    def body(front_panel, solved_prev, *rest):
        nblk, block, kc = front_panel.shape
        width = solved_prev.shape[1]
        fits = n_row == 4 and n_src % 2 == 0 and n_src >= 4 and n_src <= 16
        fits = fits and block % 32 == 0 and kc % 128 == 0 and width % 256 == 0
        if fits:
            return fast_body(n_row, n_src, front_panel, solved_prev, *rest)
        return general_body(front_panel, solved_prev, *rest)

    in_specs = (P(None, None, ("row", "src")), P("row", "src"), P(None, "src"), P(), P(), P())
    out_specs = P("row", "src")
    return jax.shard_map(body, mesh=mesh, in_specs=in_specs, out_specs=out_specs, check_vma=False)
```

```python
import functools

import jax
import jax.numpy as jnp
from jax import lax
from jax.experimental import pallas as pl
from jax.experimental.pallas import tpu as pltpu
from jax.sharding import PartitionSpec as P

F32 = jnp.float32
BF16 = jnp.bfloat16
MESH = pl.DeviceIdType.MESH


def general_body(front_panel, solved_prev, right_side, front_window, inv_diag, owner_map):
    highest = lax.Precision.HIGHEST
    nblk = front_panel.shape[0]
    block = front_panel.shape[1]
    width = solved_prev.shape[1]
    here = lax.axis_index("row")
    panel_rows = lax.all_gather(front_panel, "src", axis=2, tiled=True)
    local = jnp.einsum(
        "kbn,ns->kbs",
        panel_rows,
        solved_prev,
        precision=highest,
        preferred_element_type=jnp.float32,
    )
    partials = lax.psum(local, "row")
    stored = jnp.zeros((block, width), jnp.float32)
    solutions = []
    for k in range(nblk):
        rhs = right_side[k * block : (k + 1) * block] - partials[k]
        if k > 0:
            earlier = jnp.concatenate(solutions, axis=0)
            rhs = rhs - jnp.dot(
                front_window[k * block : (k + 1) * block, : k * block],
                earlier,
                precision=highest,
                preferred_element_type=jnp.float32,
            )
        mine = here == owner_map[k]
        solution = jnp.dot(inv_diag[k], rhs, precision=highest, preferred_element_type=jnp.float32)
        solutions.append(solution)
        stored = stored + jnp.where(mine, solution, jnp.zeros_like(solution))
    return stored


def split(v):
    hi = v.astype(BF16)
    return hi, (v - hi.astype(F32)).astype(BF16)


def dot(a, b):
    return jnp.dot(a, b, preferred_element_type=F32)


def dot3(a, b):
    (ah, al), (bh, bl) = split(a), split(b)
    return dot(ah, bh) + (dot(ah, bl) + dot(al, bh))


def kernel(
    nz, n_row, cut, owner, fp, sp, rs_hbm, win_hbm, inv_hbm, out,
    ga, rb, sv, rs, win, inv, bh, bl, acc, rc, sx, rx, ty, ry, fs, fr,
    zr_send, zl_send, z_recv, b_send, b_recv, c_send, c_recv, x_send, x_recv, y_send, y_recv, f_sem, l_sem, g_sem, s_sem,
):
    pieces, rows, kc = fp.shape
    width = sp.shape[1]
    half = width // 2
    nblk = pieces // cut
    block = rows * cut
    row, src = lax.axis_index("row"), lax.axis_index("src")
    z, x = src // 2, lax.rem(src, 2)
    core = lax.rem(row, 2)
    sib = row + 1 - 2 * core
    yp = lax.rem(row + 2, n_row)
    xp = src + 1 - 2 * x
    has_l, has_r = z > 0, z < nz - 1

    to_sib = {"row": sib, "src": src}
    to_y = {"row": yp, "src": src}
    to_x = {"row": row, "src": xp}
    to_r = {"row": row, "src": src + 2}
    to_l = {"row": row, "src": src - 2}

    def remote(s, d, ss, rr, dev):
        return pltpu.make_async_remote_copy(
            src_ref=s, dst_ref=d, send_sem=ss, recv_sem=rr, device_id=dev, device_id_type=MESH
        )

    def rows_of(o, par):
        return pl.ds(pl.multiple_of((2 * o + par) * kc, kc), kc)

    def own_copy(p):
        return pltpu.make_async_copy(fp.at[p], ga.at[p, z], g_sem.at[p])

    def sv_copy(o):
        return pltpu.make_async_copy(sp.at[rows_of(o, x)], sv.at[o], s_sem.at[o])

    small = [
        pltpu.make_async_copy(rs_hbm, rs, l_sem.at[0]),
        pltpu.make_async_copy(win_hbm, win, l_sem.at[1]),
        pltpu.make_async_copy(inv_hbm, inv, l_sem.at[2]),
    ]

    barrier = pltpu.get_barrier_semaphore()

    def hello(dev):
        pl.semaphore_signal(barrier, inc=1, device_id=dev, device_id_type=MESH)

    for dev in (to_sib, to_y, to_x):
        hello(dev)
    pl.when(has_l)(lambda: hello(to_l))
    pl.when(has_r)(lambda: hello(to_r))
    for o in range(nz):
        sv_copy(o).start()
    for p in range(pieces):
        own_copy(p).start()
    for copy in small:
        copy.start()
    pl.semaphore_wait(barrier, 3 + has_l.astype(jnp.int32) + has_r.astype(jnp.int32))

    def right(p, o, own=False):
        s = fp.at[p] if own else ga.at[p, o]
        return remote(s, ga.at[p, o], zr_send.at[p, o], z_recv.at[p, o], to_r)

    def left(p, o, own=False):
        s = fp.at[p] if own else ga.at[p, o]
        return remote(s, ga.at[p, o], zl_send.at[p, o], z_recv.at[p, o], to_l)

    def b_copy(o):
        return remote(sp.at[rows_of(o, 1 - x)], rb.at[o], b_send.at[o], b_recv.at[o], to_x)

    def passing(p, d):
        @pl.when(z - d >= 0)
        def _():
            right(p, z - d).wait_recv()
            pl.when(has_r)(lambda: right(p, z - d).start())

        @pl.when(z + d < nz)
        def _():
            left(p, z + d).wait_recv()
            pl.when(has_l)(lambda: left(p, z + d).start())

    def each(body):
        lax.fori_loop(0, pieces, lambda p, c: (body(p), c)[1], 0)

    for p in range(pieces):
        pl.when(has_r)(lambda p=p: right(p, z, True).start())
        pl.when(has_l)(lambda p=p: left(p, z, True).start())
        if p < nz:
            b_copy(p).start()
    for o in range(pieces, nz):
        b_copy(o).start()

    for o in range(nz):
        sv_copy(o).wait()
        hi, lo = split(sv[o])
        bh[0, o * kc : (o + 1) * kc] = hi
        bl[0, o * kc : (o + 1) * kc] = lo

    each(lambda p: passing(p, 1))
    for copy in small:
        copy.wait()
    for o in range(nz):
        b_copy(o).wait_recv()
        hi, lo = split(rb[o])
        bh[1, o * kc : (o + 1) * kc] = hi
        bl[1, o * kc : (o + 1) * kc] = lo

    def product(p, o, first=False):
        hi, lo = split(ga[p, o])
        at = pl.ds(pl.multiple_of(o * kc, kc), kc)
        for g in range(2):
            t = dot(hi, bh[g, at]) + (dot(hi, bl[g, at]) + dot(lo, bh[g, at]))
            if first:
                acc[p, 0, g] = t[:, :half]
                acc[p, 1, g] = t[:, half:]
            else:
                acc[p, 0, g] += t[:, :half]
                acc[p, 1, g] += t[:, half:]

    def own_product(p):
        own_copy(p).wait()
        product(p, z, True)

    def products(p, d):
        if 2 * d >= nz:
            some = (z - d >= 0) | (z + d < nz)
            pl.when(some)(lambda: product(p, jnp.where(z - d >= 0, z - d, z + d)))
        else:
            pl.when(z - d >= 0)(lambda: product(p, z - d))
            pl.when(z + d < nz)(lambda: product(p, z + d))

    each(own_product)
    each(lambda p: products(p, 1))
    for d in range(2, nz - 1):

        def both(p, d=d):
            passing(p, d)
            products(p, d)

        each(both)

    def c_copy(p):
        return remote(acc.at[p, 1 - core], rc.at[p], c_send.at[p], c_recv.at[p], to_sib)

    def x_copy(p):
        return remote(sx.at[p, 1], rx.at[p], x_send.at[p], x_recv.at[p], to_x)

    def y_copy(p):
        return remote(ty.at[p], ry.at[p], y_send.at[p], y_recv.at[p], to_y)

    cols = pl.ds(pl.multiple_of(core * half, half), half)
    other = pl.ds(pl.multiple_of((1 - core) * half, half), half)
    solutions = []
    rhs = [None]

    def stage_core(p):
        c_copy(p).wait_recv()
        sx[p, 1] = acc[p, core, 1] + rc[p, 1]
        x_copy(p).start()
        sx[p, 0] = acc[p, core, 0] + rc[p, 0]

    def stage_x(p):
        x_copy(p).wait_recv()
        ty[p] = sx[p, 0] + rx[p]
        y_copy(p).start()

    def prepare(k):
        v = rs[k * block : (k + 1) * block, cols]
        for j in range(k):
            v = v - dot3(win[k * block : (k + 1) * block, j * block : (j + 1) * block], solutions[j])
        return v

    def stage_y(p):
        y_copy(p).wait_recv()
        if p % cut == cut - 1:
            k = p // cut
            total = jnp.concatenate([ty[q] + ry[q] for q in range(k * cut, p + 1)], axis=0)
            solutions.append(dot3(inv[k], (rhs[0] if rhs[0] is not None else prepare(k)) - total))
            rhs[0] = prepare(k + 1) if k + 1 < nblk else None

    for step in range(pieces + 2):
        if step < pieces:
            if nz > 2:
                passing(step, nz - 1)
                products(step, nz - 1)
            c_copy(step).start()
            stage_core(step)
        if 0 <= step - 1 < pieces:
            stage_x(step - 1)
        if 0 <= step - 2 < pieces:
            stage_y(step - 2)

    def pick(r):
        total = jnp.zeros((block, half), F32)
        for k in range(nblk):
            total = total + jnp.where(owner[k] == r, solutions[k], jnp.zeros_like(total))
        return total

    fs[...] = pick(sib)
    final = remote(fs, fr, f_sem.at[0], f_sem.at[1], to_sib)
    final.start()
    out[:, cols] = pick(row)

    def settle(p):
        for o in range(nz):
            pl.when(has_r & (o <= z))(lambda o=o: right(p, o).wait_send())
            pl.when(has_l & (o >= z))(lambda o=o: left(p, o).wait_send())
        c_copy(p).wait_send()
        x_copy(p).wait_send()
        y_copy(p).wait_send()

    each(settle)
    for o in range(nz):
        b_copy(o).wait_send()
    final.wait()
    out[:, other] = fr[...]


def fast_body(n_row, n_src, front_panel, solved_prev, right_side, front_window, inv_diag, owner_map):
    nblk, block, kc = front_panel.shape
    width = solved_prev.shape[1]
    nz, half = n_src // 2, width // 2
    cut = 2
    pieces, rows = nblk * cut, block // cut
    hbm = pl.BlockSpec(memory_space=pl.ANY)
    dma = pltpu.SemaphoreType.DMA
    return pl.pallas_call(
        functools.partial(kernel, nz, n_row, cut),
        out_shape=jax.ShapeDtypeStruct((block, width), F32),
        in_specs=[pl.BlockSpec(memory_space=pltpu.SMEM)] + [hbm] * 5,
        out_specs=pl.BlockSpec(memory_space=pltpu.VMEM),
        scratch_shapes=[
            pltpu.VMEM((pieces, nz, rows, kc), F32),
            pltpu.VMEM((nz, kc, width), F32),
            pltpu.VMEM((nz, kc, width), F32),
            pltpu.VMEM(right_side.shape, F32),
            pltpu.VMEM(front_window.shape, F32),
            pltpu.VMEM(inv_diag.shape, F32),
            pltpu.VMEM((2, nz * kc, width), BF16),
            pltpu.VMEM((2, nz * kc, width), BF16),
            pltpu.VMEM((pieces, 2, 2, rows, half), F32),
            pltpu.VMEM((pieces, 2, rows, half), F32),
            pltpu.VMEM((pieces, 2, rows, half), F32),
            pltpu.VMEM((pieces, rows, half), F32),
            pltpu.VMEM((pieces, rows, half), F32),
            pltpu.VMEM((pieces, rows, half), F32),
            pltpu.VMEM((block, half), F32),
            pltpu.VMEM((block, half), F32),
            dma((pieces, nz)),
            dma((pieces, nz)),
            dma((pieces, nz)),
            dma((nz,)),
            dma((nz,)),
            dma((pieces,)),
            dma((pieces,)),
            dma((pieces,)),
            dma((pieces,)),
            dma((pieces,)),
            dma((pieces,)),
            dma((2,)),
            dma((3,)),
            dma((pieces,)),
            dma((nz,)),
        ],
        compiler_params=pltpu.CompilerParams(
            collective_id=0, has_side_effects=True, vmem_limit_bytes=56 * 2**20
        ),
    )(
        owner_map, front_panel.reshape(pieces, rows, kc), solved_prev, right_side, front_window, inv_diag
    )


def solution(mesh):
    n_row, n_src = mesh.shape["row"], mesh.shape["src"]

    def body(front_panel, solved_prev, *rest):
        nblk, block, kc = front_panel.shape
        width = solved_prev.shape[1]
        fits = n_row == 4 and n_src % 2 == 0 and n_src >= 4 and n_src <= 16
        fits = fits and block % 32 == 0 and kc % 128 == 0 and width % 256 == 0
        if fits:
            return fast_body(n_row, n_src, front_panel, solved_prev, *rest)
        return general_body(front_panel, solved_prev, *rest)

    in_specs = (P(None, None, ("row", "src")), P("row", "src"), P(None, "src"), P(), P(), P())
    out_specs = P("row", "src")
    return jax.shard_map(body, mesh=mesh, in_specs=in_specs, out_specs=out_specs, check_vma=False)
```
